32 devices in a mesh: gx: 4 (over y, core), gy: 8 (over z, x).
Axes of the slice: x: 2, y: 2, z: 4, core: 2. Of those that a mesh axis runs over, the one named last changes fastest.
Arguments:
- patches: bfloat16 [2048, 1664], P(('gx', 'gy')), may hold values from -6 to 6
- prompt: bfloat16 [2560, 1664], P(('gx', 'gy')), may hold values from -6 to 6
- image_ids: int32 [4, 128], P('gx'), may hold values from 0 to 3, never falling along the last dimension, each value on 1 to 64 neighbouring positions
- positions: int32 [4, 128], P('gx'), may hold values from 0 to 639, as said below
- norm_gains: float32 [5, 1664], replicated, may hold values from 0.25 to 1.75
- vit_qkv: bfloat16 [1664, 4992], P('gx', 'gy'), may hold values from -0.24514517 to 0.24514517
- vit_out: bfloat16 [1664, 1664], P('gx', 'gy'), may hold values from -0.15625 to 0.15625
- vit_up: bfloat16 [1664, 8192], P('gx', 'gy'), may hold values from -0.15625 to 0.15625
- vit_down: bfloat16 [1664, 8192], P('gx', 'gy'), may hold values from -0.0625 to 0.0625
- merge_proj: bfloat16 [6656, 1664], P('gx', 'gy'), may hold values from -0.078125 to 0.078125
- dec_qkv: bfloat16 [1664, 4992], P('gx', 'gy'), may hold values from -0.24514517 to 0.24514517
- dec_out: bfloat16 [1664, 1664], P('gx', 'gy'), may hold values from -0.15625 to 0.15625
- dec_up: bfloat16 [1664, 8192], P('gx', 'gy'), may hold values from -0.15625 to 0.15625
- dec_down: bfloat16 [1664, 8192], P('gx', 'gy'), may hold values from -0.0625 to 0.0625
Outputs:
- decoded: bfloat16 [2560, 1664], P(('gx', 'gy'))
The draws below stay inside these ranges and needn't reach their ends.
Inputs may be any that keep to these rules, and one draw needn't show every extreme that they name: `image_ids`: within each sequence image numbers never fall, and each of the 4 images has at least one merged row. Within each sequence the positions strictly increase.
All inputs are finite; a program needn't handle non-finite values.
Results may differ from the reference program's by a relative error of at most 0.03.
Values may be sent and summed in bfloat16 or wider, within the bound.
No kernel may reach another device: no remote copies, remote signals or barrier semaphores. Data moves between devices by JAX's collectives and lax.ppermute only.
A program may use at most 64 MiB of HBM per device.

```python
import math
import jax
import jax.numpy as jnp
import numpy as np
from jax import lax

D = 1664
HEADS = 16
HEAD_DIM = 104
FF = 8192
PATCH_DEV = 64
IMAGES = 4
BATCH = 4
MERGED_G = 128
TEXT_G = 512
SEQ_G = 640
PATCHES = 2048
SEQ_ALL = 2560
N_GY = 8


def clipped_normal(key, salt, shape):
    return jnp.clip(jax.random.normal(jax.random.fold_in(key, salt), shape, jnp.float32), -6.0, 6.0)


def merged_spots(key):
    gaps = jax.random.randint(jax.random.fold_in(key, 11), (BATCH, MERGED_G), 0, TEXT_G + 1, dtype=jnp.int32)
    gaps = jnp.sort(gaps, axis=1)
    gaps = gaps.at[:, MERGED_G - 1].set(TEXT_G)
    gaps = gaps.at[0, 0].set(0)
    return (gaps + jnp.arange(MERGED_G, dtype=jnp.int32)[None, :]).astype(jnp.int32)


def draw_positions(key, part):
    return merged_spots(key)


def draw_patches(key, part):
    values = clipped_normal(key, 21, (PATCHES, D))
    return values.astype(jnp.bfloat16)


def draw_prompt(key, part):
    values = clipped_normal(key, 31, (SEQ_ALL, D))
    return values.astype(jnp.bfloat16)


def draw_vit_qkv(key, part):
    values = clipped_normal(key, 41, (D, 3 * D)) * D ** (-0.5)
    return values.astype(jnp.bfloat16)


def draw_dec_qkv(key, part):
    values = clipped_normal(key, 51, (D, 3 * D)) * D ** (-0.5)
    return values.astype(jnp.bfloat16)


def block_levels(key, shape, cuts, least, largest):
    factor_of = 1.0
    for axis_at, shards_of in cuts:
        draws = jax.random.uniform(jax.random.fold_in(jax.random.fold_in(key, 6), axis_at), (shards_of,), jnp.float32, least / len(cuts), largest / len(cuts))
        factor_of = factor_of * jnp.repeat(jnp.exp(draws), shape[axis_at] // shards_of).reshape((-1,) + (1,) * (len(shape) - 1 - axis_at))
    return factor_of


def profile(amount, total, reach, skew):
    portions = [(1 << 20) // math.isqrt(grade ** skew) + 1 for grade in range(2, amount + 1)]
    rest, counts = total - reach - (amount - 1), [1] * (amount - 1)
    while rest > 0:
        movable = [i for i in range(amount - 1) if counts[i] < reach]
        pool, remaining = sum([portions[i] for i in movable]), rest
        for i in movable:
            addition = min(reach - counts[i], max(1, remaining * portions[i] // pool), rest)
            counts[i] = counts[i] + addition
            rest = rest - addition
    return np.array([reach] + counts)


def ragged_sizes(own_key, count, total, reach, slope):
    if count == 2:
        one = jax.random.randint(own_key, (), max(1, total - reach), min(reach, total - 1) + 1)
        return jnp.stack([one, total - one])
    tallies = jnp.asarray(profile(count, total, reach, slope), jnp.int32)
    pairs = (count - 1) // 2
    giver, taker = tallies[1:1 + 2 * pairs:2], tallies[2:2 + 2 * pairs:2]
    slack = jnp.minimum(giver - 1, reach - taker)
    passed = jax.random.randint(jax.random.fold_in(own_key, 1), (pairs,), 0, 1 << 20) % (slack + 1)
    tallies = tallies.at[1:1 + 2 * pairs:2].set(giver - passed).at[2:2 + 2 * pairs:2].set(taker + passed)
    return tallies[jax.random.permutation(jax.random.fold_in(own_key, 2), count)]


def bell_draw(rng, shape, scale, limit, shards=(), kind=jnp.bfloat16):
    entries = jax.random.normal(rng, shape, jnp.float32) * scale
    if len(shards) > 0:
        entries = block_levels(rng, shape, shards, -0.22, 0.18) * entries
    return jnp.clip(entries, min=-limit, max=limit).astype(kind)


def setup_inputs(seed: int = 0) -> dict:
    splits = jax.random.split(jax.random.key(seed), 15)
    return {
        "patches": draw_patches(jax.random.fold_in(splits[14], 71), 0),
        "prompt": draw_prompt(jax.random.fold_in(splits[14], 71), 0),
        "image_ids": jax.vmap(lambda own: jnp.searchsorted(jnp.cumsum(ragged_sizes(own, IMAGES, MERGED_G, MERGED_G // 2, 1)), jnp.arange(MERGED_G), side="right"))(jax.random.split(splits[2], BATCH)).reshape((BATCH, MERGED_G)).astype(jnp.int32),
        "positions": draw_positions(jax.random.fold_in(splits[14], 71), 0),
        "norm_gains": jnp.clip(1.0 + 0.15 * jax.random.normal(splits[4], (5, D), jnp.float32), 0.25, 1.75),
        "vit_qkv": draw_vit_qkv(jax.random.fold_in(splits[14], 71), 0),
        "vit_out": bell_draw(splits[6], (D, D), D ** -0.5, 0.15625, ((0, 4), (1, 8))),
        "vit_up": bell_draw(splits[7], (D, FF), D ** -0.5, 0.15625, ((0, 4), (1, 8))),
        "vit_down": bell_draw(splits[8], (D, FF), FF ** -0.5, 0.0625, ((0, 4), (1, 8))),
        "merge_proj": bell_draw(splits[9], (4 * D, D), (4 * D) ** -0.5, 0.078125, ((0, 4), (1, 8))),
        "dec_qkv": draw_dec_qkv(jax.random.fold_in(splits[14], 71), 0),
        "dec_out": bell_draw(splits[11], (D, D), D ** -0.5, 0.15625, ((0, 4), (1, 8))),
        "dec_up": bell_draw(splits[12], (D, FF), D ** -0.5, 0.15625, ((0, 4), (1, 8))),
        "dec_down": bell_draw(splits[13], (D, FF), FF ** -0.5, 0.0625, ((0, 4), (1, 8))),
    }


def layer_norm(rows, gain):
    values = rows.astype(jnp.float32)
    center = values - lax.optimization_barrier(jnp.mean(values, axis=-1, keepdims=True))
    spread = lax.optimization_barrier(jnp.mean(center * center, axis=-1, keepdims=True))
    return center * lax.rsqrt(spread + 1e-06) * gain

def rms_norm(rows, gain):
    values = rows.astype(jnp.float32)
    return values * lax.rsqrt(lax.optimization_barrier(jnp.mean(values * values, axis=-1, keepdims=True)) + 1e-06) * gain

def blocked(hidden, weight):
    total = hidden.shape[0]
    width = hidden.shape[1]
    outer = weight.shape[0]
    left = hidden.astype(jnp.float32).reshape(total, N_GY, width // N_GY)
    right = weight.astype(jnp.float32).reshape(outer, N_GY, width // N_GY)
    parts = jnp.einsum('rjc,djc->jrd', left, right).astype(jnp.bfloat16)
    parts = lax.optimization_barrier(parts)
    return lax.optimization_barrier(jnp.sum(parts.astype(jnp.float32), axis=0))

def attend(joined, allowed):
    total = joined.shape[0]
    grouped = joined.astype(jnp.float32).reshape(total, HEADS, 3, HEAD_DIM)
    query = grouped[:, :, 0]
    keys = grouped[:, :, 1]
    values = grouped[:, :, 2]
    scores = jnp.einsum('qhe,khe->hqk', query, keys) * (1.0 / math.sqrt(HEAD_DIM))
    scores = jnp.where(allowed[None], scores, -1e+30)
    top = lax.optimization_barrier(jnp.max(scores, axis=-1, keepdims=True))
    weights = jnp.exp(scores - top)
    probs = (weights / lax.optimization_barrier(jnp.sum(weights, axis=-1, keepdims=True))).astype(jnp.bfloat16)
    probs = lax.optimization_barrier(probs)
    mixed = jnp.einsum('hqk,khe->qhe', probs.astype(jnp.float32), values)
    return mixed.astype(jnp.bfloat16).reshape(total, HEADS * HEAD_DIM)

def reference(patches, prompt, image_ids, positions, norm_gains, vit_qkv, vit_out, vit_up, vit_down, merge_proj, dec_qkv, dec_out, dec_up, dec_down):
    patch_rows = PATCH_DEV * N_GY

    def one_sequence(inputs):
        seq_patches, seq_prompt, seq_ids, seq_pos = inputs
        labels = jnp.repeat(seq_ids, 4)
        enc_in = layer_norm(seq_patches, norm_gains[0]).astype(jnp.bfloat16)
        enc_qkv = jnp.dot(enc_in, vit_qkv, preferred_element_type=jnp.float32).astype(jnp.bfloat16)
        enc_mix = attend(enc_qkv, labels[:, None] == labels[None, :])
        enc_mid = (seq_patches.astype(jnp.float32) + blocked(enc_mix, vit_out)).astype(jnp.bfloat16)
        normed = layer_norm(enc_mid, norm_gains[1]).astype(jnp.bfloat16)
        enc_hidden = jax.nn.gelu(jnp.dot(normed, vit_up, preferred_element_type=jnp.float32), approximate=False).astype(jnp.bfloat16)
        enc_out = (enc_mid.astype(jnp.float32) + blocked(enc_hidden, vit_down)).astype(jnp.bfloat16)
        windows = layer_norm(enc_out, norm_gains[2]).astype(jnp.bfloat16).reshape(patch_rows // 4, 4 * D)
        merged = jnp.dot(windows, merge_proj, preferred_element_type=jnp.float32).astype(jnp.bfloat16)
        spots = jnp.arange(SEQ_G, dtype=jnp.int32)
        hits = seq_pos[None, :] == spots[:, None]
        placed = jnp.dot(hits.astype(jnp.bfloat16), merged, preferred_element_type=jnp.float32).astype(jnp.bfloat16)
        dec_in = jnp.where(jnp.any(hits, axis=1)[:, None], placed, seq_prompt)
        dnormed = rms_norm(dec_in, norm_gains[3]).astype(jnp.bfloat16)
        dec_rows = jnp.dot(dnormed, dec_qkv, preferred_element_type=jnp.float32).astype(jnp.bfloat16)
        dec_mix = attend(dec_rows, spots[:, None] >= spots[None, :])
        dec_mid = (dec_in.astype(jnp.float32) + blocked(dec_mix, dec_out)).astype(jnp.bfloat16)
        enormed = rms_norm(dec_mid, norm_gains[4]).astype(jnp.bfloat16)
        dec_hidden = jax.nn.gelu(jnp.dot(enormed, dec_up, preferred_element_type=jnp.float32), approximate=False).astype(jnp.bfloat16)
        return (dec_mid.astype(jnp.float32) + blocked(dec_hidden, dec_down)).astype(jnp.bfloat16)
    outputs = lax.map(one_sequence, (patches.reshape(BATCH, patch_rows, D), prompt.reshape(BATCH, SEQ_G, D), image_ids, positions))
    return outputs.reshape(BATCH * SEQ_G, D)
```

```python
import math

import jax
import jax.numpy as jnp
from jax import lax
from jax.sharding import PartitionSpec as P

HEAD_DIM = 104
BF = jnp.bfloat16
F32 = jnp.float32


def layer_norm(rows, gain):
    values = rows.astype(F32)
    center = values - jnp.mean(values, axis=-1, keepdims=True)
    spread = jnp.mean(center * center, axis=-1, keepdims=True)
    return center * lax.rsqrt(spread + 1e-06) * gain


def rms_norm(rows, gain):
    values = rows.astype(F32)
    return values * lax.rsqrt(jnp.mean(values * values, axis=-1, keepdims=True) + 1e-06) * gain


def grid_of(count):
    fast = 2 ** ((count.bit_length() - 1) // 2)
    return count // fast, fast


def moved(value, dz, dx):
    nz, nx = grid_of(lax.axis_size("gy"))
    pairs = [
        (z * nx + x, ((z + dz) % nz) * nx + (x + dx) % nx) for z in range(nz) for x in range(nx)
    ]
    return lax.ppermute(value, "gy", pairs)


def far_first(nz):
    return sorted(range(1, nz), key=lambda k: -min(k, nz - k))


def relative_blocks(value):
    nz, nx = grid_of(lax.axis_size("gy"))
    found = {(0, 0): value}
    for k in far_first(nz):
        found[k, 0] = moved(value, -k, 0)
    for k in [0] + sorted(range(1, nz), key=lambda k: min(k, nz - k)):
        for p in range(1, nx):
            found[k, p] = moved(found[k, 0], 0, -p)
    return [found[k, p] for k in range(nz) for p in range(nx)]


def relative_gather(value):
    return jnp.concatenate(relative_blocks(value), axis=0)


def relative_owner():
    nz, nx = grid_of(lax.axis_size("gy"))
    me = lax.axis_index("gy")
    z, x = me // nx, me % nx
    return jnp.stack([((z + k) % nz) * nx + (x + p) % nx for k in range(nz) for p in range(nx)])


def relative_scatter(term, local):
    nz, nx = grid_of(lax.axis_size("gy"))
    pieces = {
        (k, p): term[(k * nx + p) * local : (k * nx + p + 1) * local]
        for k in range(nz)
        for p in range(nx)
    }
    sums = {}
    for k in far_first(nz) + [0]:
        total = pieces[k, 0].astype(F32)
        for p in range(1, nx):
            total = total + moved(pieces[k, p], 0, p).astype(F32)
        sums[k] = total
    out = sums[0]
    for k in far_first(nz):
        out = out + moved(sums[k].astype(BF), k, 0).astype(F32)
    return out


def absolute_rows(value):
    nz, nx = grid_of(lax.axis_size("gy"))
    me = lax.axis_index("gy")
    z, x = me // nx, me % nx
    blocks = value.reshape(nz, nx, value.shape[0] // (nz * nx), value.shape[1])
    blocks = lax.dynamic_slice_in_dim(jnp.concatenate([blocks] * 2, 0), (nz - z) % nz, nz, 0)
    blocks = lax.dynamic_slice_in_dim(jnp.concatenate([blocks] * 2, 1), (nx - x) % nx, nx, 1)
    return blocks.reshape(value.shape)


def small_weight(weight):
    count = lax.axis_size("gx")
    me = lax.axis_index("gx")
    rows = weight.shape[0]
    whole = jnp.zeros((rows * count, weight.shape[1]), weight.dtype)
    for j in range(count // 2):
        along = weight
        if j:
            along = lax.ppermute(weight, "gx", [(i, (i - 2 * j) % count) for i in range(count)])
        other = lax.ppermute(along, "gx", [(i, i ^ 1) for i in range(count)])
        spot = (me + 2 * j) % count
        whole = lax.dynamic_update_slice(whole, along, (spot * rows, 0))
        whole = lax.dynamic_update_slice(whole, other, ((spot ^ 1) * rows, 0))
    return whole


def weight_block(weight):
    return lax.all_gather(weight, "gx", axis=0, tiled=True)


def tied(first, *later):
    return lax.optimization_barrier((first, *later))


def attend(joined, allowed):
    total = joined.shape[0]
    heads_here = joined.shape[1] // (3 * HEAD_DIM)
    grouped = joined.reshape(total, heads_here, 3, HEAD_DIM)
    query = grouped[:, :, 0]
    keys = grouped[:, :, 1]
    values = grouped[:, :, 2]
    scale = 1.0 / math.sqrt(HEAD_DIM)
    scores = jnp.einsum("qhe,khe->hqk", query, keys, preferred_element_type=F32) * scale
    scores = jnp.where(allowed[None], scores, -1e30)
    top = jnp.max(scores, axis=-1, keepdims=True)
    weights = jnp.exp(scores - top)
    probs = (weights / jnp.sum(weights, axis=-1, keepdims=True)).astype(BF)
    mixed = jnp.einsum("hqk,khe->qhe", probs, values, preferred_element_type=F32)
    return mixed.astype(BF).reshape(total, heads_here * HEAD_DIM)


def out_term(hidden, weight):
    return lax.dot_general(
        hidden, weight, (((1,), (1,)), ((), ())), preferred_element_type=F32
    ).astype(BF)


def shards(
    patches,
    prompt,
    image_ids,
    positions,
    norm_gains,
    vit_qkv,
    vit_out,
    vit_up,
    vit_down,
    merge_proj,
    dec_qkv,
    dec_out,
    dec_up,
    dec_down,
):
    local = patches.shape[0]
    width = patches.shape[1]
    seq_local = prompt.shape[0]
    owner = relative_owner()
    rows_of = (owner[:, None] * local + jnp.arange(local, dtype=jnp.int32)).reshape(-1)
    spots_of = (owner[:, None] * seq_local + jnp.arange(seq_local, dtype=jnp.int32)).reshape(-1)
    labels = image_ids[0][rows_of // 4]

    qkv_block = weight_block(vit_qkv)
    enc_in = relative_gather(layer_norm(patches, norm_gains[0]).astype(BF))
    enc_qkv = jnp.dot(enc_in, qkv_block, preferred_element_type=F32).astype(BF)
    out_block = small_weight(vit_out)
    enc_qkv, out_block, vit_up = tied(enc_qkv, out_block, vit_up)
    enc_mix = attend(enc_qkv, labels[:, None] == labels[None, :])
    summed = relative_scatter(out_term(enc_mix, out_block), local)
    enc_mid = (patches.astype(F32) + summed).astype(BF)
    up_block = weight_block(vit_up)
    enc_mid, up_block, vit_down = tied(enc_mid, up_block, vit_down)

    down_block = weight_block(vit_down)
    normed = relative_gather(layer_norm(enc_mid, norm_gains[1]).astype(BF))
    normed, down_block, merge_proj, prompt = tied(normed, down_block, merge_proj, prompt)
    merge_block = weight_block(merge_proj)
    hidden = jax.nn.gelu(
        jnp.dot(normed, up_block, preferred_element_type=F32), approximate=False
    ).astype(BF)
    summed = relative_scatter(out_term(hidden, down_block), local)
    enc_out = (enc_mid.astype(F32) + summed).astype(BF)
    enc_out, merge_block, dec_qkv = tied(enc_out, merge_block, dec_qkv)

    dqkv_block = weight_block(dec_qkv)
    windows = layer_norm(enc_out, norm_gains[2]).astype(BF).reshape(local // 4, 4 * width)
    windows = relative_gather(windows)
    prompt_all = relative_gather(prompt)
    merged = jnp.dot(windows, merge_block, preferred_element_type=F32).astype(BF)
    merged, dqkv_block, dec_up = tied(merged, dqkv_block, dec_up)
    merged_all = lax.all_gather(absolute_rows(merged), "gy", axis=1, tiled=True)
    hits = positions[0][None, :] == spots_of[:, None]
    placed = jnp.dot(hits.astype(BF), merged_all, preferred_element_type=F32).astype(BF)
    dec_all = jnp.where(jnp.any(hits, axis=1)[:, None], placed, prompt_all)
    dec_in = dec_all[:seq_local]

    dup_block = weight_block(dec_up)
    dout_block = small_weight(dec_out)
    dnormed = rms_norm(dec_all, norm_gains[3]).astype(BF)
    dec_rows = jnp.dot(dnormed, dqkv_block, preferred_element_type=F32).astype(BF)
    dec_mix = attend(dec_rows, spots_of[:, None] >= spots_of[None, :])
    summed = relative_scatter(out_term(dec_mix, dout_block), seq_local)
    dec_mid = (dec_in.astype(F32) + summed).astype(BF)
    dec_mid, dup_block, dec_down = tied(dec_mid, dup_block, dec_down)

    ddown_block = weight_block(dec_down)
    enormed = relative_gather(rms_norm(dec_mid, norm_gains[4]).astype(BF))
    dec_hidden = jax.nn.gelu(
        jnp.dot(enormed, dup_block, preferred_element_type=F32), approximate=False
    ).astype(BF)
    summed = relative_scatter(out_term(dec_hidden, ddown_block), seq_local)
    return (dec_mid.astype(F32) + summed).astype(BF)


def solution(mesh):
    weight = P("gx", "gy")
    rows = P(("gx", "gy"), None)
    in_specs = (rows, rows, P("gx", None), P("gx", None), P()) + (weight,) * 9
    return jax.shard_map(shards, mesh=mesh, in_specs=in_specs, out_specs=rows, check_vma=False)
```

```python
import math

import jax
import jax.numpy as jnp
from jax import lax
from jax.sharding import PartitionSpec as P

HEAD_DIM = 104
BF = jnp.bfloat16
F32 = jnp.float32


def layer_norm(rows, gain):
    values = rows.astype(F32)
    center = values - jnp.mean(values, axis=-1, keepdims=True)
    spread = jnp.mean(center * center, axis=-1, keepdims=True)
    return center * lax.rsqrt(spread + 1e-06) * gain


def rms_norm(rows, gain):
    values = rows.astype(F32)
    return values * lax.rsqrt(jnp.mean(values * values, axis=-1, keepdims=True) + 1e-06) * gain


def grid_of(count):
    fast = 2 ** ((count.bit_length() - 1) // 2)
    return count // fast, fast


def moved(value, dz, dx):
    nz, nx = grid_of(lax.axis_size("gy"))
    pairs = [
        (z * nx + x, ((z + dz) % nz) * nx + (x + dx) % nx) for z in range(nz) for x in range(nx)
    ]
    return lax.ppermute(value, "gy", pairs)


def z_order(nz):
    return sorted(range(nz), key=lambda k: (min(k, nz - k), k))


def start_gather(value):
    nz, nx = grid_of(lax.axis_size("gy"))
    found = {(0, 0): value}
    for k in z_order(nz)[1:]:
        found[k, 0] = moved(value, -k, 0)
    for p in range(1, nx):
        found[0, p] = moved(value, 0, -p)
    return found


def finish_gather(found):
    nz, nx = grid_of(lax.axis_size("gy"))
    order = z_order(nz)
    for k in order[1:]:
        for p in range(1, nx):
            found[k, p] = moved(found[k, 0], 0, -p)
    return jnp.concatenate([found[k, p] for k in order for p in range(nx)], axis=0)


def relative_gather(value):
    return finish_gather(start_gather(value))


def relative_owner():
    nz, nx = grid_of(lax.axis_size("gy"))
    me = lax.axis_index("gy")
    z, x = me // nx, me % nx
    return jnp.stack([((z + k) % nz) * nx + (x + p) % nx for k in z_order(nz) for p in range(nx)])


def relative_scatter(term):
    nz, nx = grid_of(lax.axis_size("gy"))
    order = z_order(nz)
    rows = term.shape[0] // (nz * nx)
    arrived, own = [], None
    for at in reversed(range(nz)):
        k = order[at]
        first = at * nx * rows
        total = term[first : first + rows].astype(F32)
        for p in range(1, nx):
            total = total + moved(term[first + p * rows : first + (p + 1) * rows], 0, p).astype(F32)
        if k:
            arrived.append(moved(total.astype(BF), k, 0))
        else:
            own = total
    for value in arrived:
        own = own + value.astype(F32)
    return own


def absolute_rows(value):
    nz, nx = grid_of(lax.axis_size("gy"))
    me = lax.axis_index("gy")
    z, x = me // nx, me % nx
    blocks = value.reshape(nz, nx, value.shape[0] // (nz * nx), value.shape[1])
    order = z_order(nz)
    turn = [order.index(k) for k in range(nz)]
    blocks = jnp.stack([blocks[at] for at in turn + turn])
    blocks = lax.dynamic_slice_in_dim(blocks, (nz - z) % nz, nz, 0)
    blocks = lax.dynamic_slice_in_dim(jnp.concatenate([blocks] * 2, 1), (nx - x) % nx, nx, 1)
    return blocks.reshape(value.shape)


def early_weight(weight):
    count = lax.axis_size("gx")
    me = lax.axis_index("gx")
    rows = weight.shape[0]
    found = {}
    for j in range(count // 2):
        along = weight
        if j:
            along = lax.ppermute(weight, "gx", [(i, (i - 2 * j) % count) for i in range(count)])
        found[j] = along, lax.ppermute(along, "gx", [(i, i ^ 1) for i in range(count)])
    whole = jnp.zeros((rows * count, weight.shape[1]), weight.dtype)
    for j in range(count // 2):
        spot = (me + 2 * j) % count
        whole = lax.dynamic_update_slice(whole, found[j][0], (spot * rows, 0))
        whole = lax.dynamic_update_slice(whole, found[j][1], ((spot ^ 1) * rows, 0))
    return whole


def weight_block(weight):
    return lax.all_gather(weight, "gx", axis=0, tiled=True)


def tied(first, *later):
    return lax.optimization_barrier((first, *later))


def attend(joined, allowed):
    total = joined.shape[0]
    heads_here = joined.shape[1] // (3 * HEAD_DIM)
    grouped = joined.reshape(total, heads_here, 3, HEAD_DIM)
    query = grouped[:, :, 0]
    keys = grouped[:, :, 1]
    values = grouped[:, :, 2]
    scale = 1.0 / math.sqrt(HEAD_DIM)
    scores = jnp.einsum("qhe,khe->hqk", query, keys, preferred_element_type=F32) * scale
    scores = jnp.where(allowed[None], scores, -1e30)
    top = jnp.max(scores, axis=-1, keepdims=True)
    weights = jnp.exp(scores - top)
    probs = (weights / jnp.sum(weights, axis=-1, keepdims=True)).astype(BF)
    mixed = jnp.einsum("hqk,khe->qhe", probs, values, preferred_element_type=F32)
    return mixed.astype(BF).reshape(total, heads_here * HEAD_DIM)


def out_term(hidden, weight):
    return lax.dot_general(
        hidden, weight, (((1,), (1,)), ((), ())), preferred_element_type=F32
    ).astype(BF)


def shards(
    patches,
    prompt,
    image_ids,
    positions,
    norm_gains,
    vit_qkv,
    vit_out,
    vit_up,
    vit_down,
    merge_proj,
    dec_qkv,
    dec_out,
    dec_up,
    dec_down,
):
    local, width = patches.shape
    seq_local = prompt.shape[0]
    merged_rows = image_ids.shape[1]
    owner = relative_owner()
    window_of = (
        owner[:, None] * (local // 4) + jnp.arange(local // 4, dtype=jnp.int32)[None, :]
    ).reshape(-1)
    picks = window_of[:, None] == jnp.arange(merged_rows, dtype=jnp.int32)[None, :]
    labels = jnp.repeat(jnp.sum(jnp.where(picks, image_ids[0][None, :], 0), axis=1), 4)
    spots_of = (
        owner[:, None] * seq_local + jnp.arange(seq_local, dtype=jnp.int32)[None, :]
    ).reshape(-1)
    hits = positions[0][None, :] == spots_of[:, None]

    patch_found = start_gather(patches)
    qkv_block = early_weight(vit_qkv)
    outs_block = weight_block(jnp.concatenate([vit_out, dec_out], axis=1))
    patch_all = finish_gather(patch_found)
    enc_in = layer_norm(patch_all, norm_gains[0]).astype(BF)
    enc_qkv = jnp.dot(enc_in, qkv_block, preferred_element_type=F32).astype(BF)
    enc_qkv, outs_block, vit_up, prompt = tied(enc_qkv, outs_block, vit_up, prompt)
    up_block = weight_block(vit_up)
    columns = vit_out.shape[1]
    out_block, dout_block = outs_block[:, :columns], outs_block[:, columns:]
    prompt_found = start_gather(prompt)
    enc_mix = attend(enc_qkv, labels[:, None] == labels[None, :])
    enc_mix, vit_down = tied(enc_mix, vit_down)
    down_block = early_weight(vit_down)
    summed = relative_scatter(out_term(enc_mix, out_block))
    enc_mid = (patches.astype(F32) + summed).astype(BF)
    enc_mid, up_block, merge_proj = tied(enc_mid, up_block, merge_proj)
    merge_block = weight_block(merge_proj)

    mid_all = relative_gather(enc_mid)
    hidden = jax.nn.gelu(
        jnp.dot(
            layer_norm(mid_all, norm_gains[1]).astype(BF), up_block, preferred_element_type=F32
        ),
        approximate=False,
    ).astype(BF)
    enc_out = (enc_mid.astype(F32) + relative_scatter(out_term(hidden, down_block))).astype(BF)
    enc_out, merge_block, dec_qkv = tied(enc_out, merge_block, dec_qkv)
    dqkv_block = weight_block(dec_qkv)
    windows = layer_norm(enc_out, norm_gains[2]).astype(BF).reshape(local // 4, 4 * width)
    windows = relative_gather(windows)
    prompt_all = finish_gather(prompt_found)
    merged = lax.dot_general(
        merge_block, windows, (((0,), (1,)), ((), ())), preferred_element_type=F32
    ).astype(BF)
    merged, dqkv_block, dec_up, dec_down = tied(merged, dqkv_block, dec_up, dec_down)
    dup_block = weight_block(dec_up)
    merged = jnp.dot(merged, picks.astype(BF), preferred_element_type=F32).astype(BF)
    merged_all = absolute_rows(relative_gather(merged))

    placed = lax.dot_general(
        hits.astype(BF), merged_all, (((1,), (1,)), ((), ())), preferred_element_type=F32
    ).astype(BF)
    dec_all = jnp.where(jnp.any(hits, axis=1)[:, None], placed, prompt_all)
    dec_in = dec_all[:seq_local]
    dnormed = rms_norm(dec_all, norm_gains[3]).astype(BF)
    dec_rows = jnp.dot(dnormed, dqkv_block, preferred_element_type=F32).astype(BF)
    dec_mix = attend(dec_rows, spots_of[:, None] >= spots_of[None, :])
    summed = relative_scatter(out_term(dec_mix, dout_block))
    dec_mid = (dec_in.astype(F32) + summed).astype(BF)
    ddown_block = early_weight(dec_down)

    mid_all = relative_gather(dec_mid)
    hidden = jax.nn.gelu(
        jnp.dot(
            rms_norm(mid_all, norm_gains[4]).astype(BF), dup_block, preferred_element_type=F32
        ),
        approximate=False,
    ).astype(BF)
    return (dec_mid.astype(F32) + relative_scatter(out_term(hidden, ddown_block))).astype(BF)


def solution(mesh):
    weight = P("gx", "gy")
    rows = P(("gx", "gy"), None)
    in_specs = (rows, rows, P("gx", None), P("gx", None), P()) + (weight,) * 9
    return jax.shard_map(shards, mesh=mesh, in_specs=in_specs, out_specs=rows, check_vma=False)
```

```python
import functools
import math

import jax
import jax.numpy as jnp
from jax import lax
from jax.experimental import pallas as pl
from jax.experimental.pallas import tpu as pltpu
from jax.sharding import PartitionSpec as P

HEAD_DIM = 104
BF = jnp.bfloat16
F32 = jnp.float32


def layer_norm(rows, gain):
    values = rows.astype(F32)
    center = values - jnp.mean(values, axis=-1, keepdims=True)
    spread = jnp.mean(center * center, axis=-1, keepdims=True)
    return center * lax.rsqrt(spread + 1e-06) * gain


def rms_norm(rows, gain):
    values = rows.astype(F32)
    return values * lax.rsqrt(jnp.mean(values * values, axis=-1, keepdims=True) + 1e-06) * gain


def grid_of(count):
    fast = 2 ** ((count.bit_length() - 1) // 2)
    return count // fast, fast


def moved(value, dz, dx):
    nz, nx = grid_of(lax.axis_size("gy"))
    pairs = [
        (z * nx + x, ((z + dz) % nz) * nx + (x + dx) % nx) for z in range(nz) for x in range(nx)
    ]
    return lax.ppermute(value, "gy", pairs)


def z_order(nz):
    return sorted(range(nz), key=lambda k: (min(k, nz - k), k))


def start_z(value):
    nz, nx = grid_of(lax.axis_size("gy"))
    found = {(0, 0): value}
    for k in z_order(nz)[1:]:
        found[k, 0] = moved(value, -k, 0)
    return found


def swap_x(found, half):
    nz, nx = grid_of(lax.axis_size("gy"))
    found = dict(found)
    for k in z_order(nz)[half * nz // 2 : (half + 1) * nz // 2]:
        for p in range(1, nx):
            found[k, p] = moved(found[k, 0], 0, -p)
    return found


def joined_blocks(found):
    nz, nx = grid_of(lax.axis_size("gy"))
    return jnp.concatenate([found[k, p] for k in z_order(nz) for p in range(nx)], axis=0)


def start_gather(value):
    nz, nx = grid_of(lax.axis_size("gy"))
    found = start_z(value)
    for p in range(1, nx):
        found[0, p] = moved(value, 0, -p)
    return found


def finish_gather(found):
    nz, nx = grid_of(lax.axis_size("gy"))
    found = dict(found)
    for k in z_order(nz)[1:]:
        for p in range(1, nx):
            found[k, p] = moved(found[k, 0], 0, -p)
    return joined_blocks(found)


def relative_gather(value):
    return finish_gather(start_gather(value))


def relative_owner():
    nz, nx = grid_of(lax.axis_size("gy"))
    me = lax.axis_index("gy")
    z, x = me // nx, me % nx
    return jnp.stack([((z + k) % nz) * nx + (x + p) % nx for k in z_order(nz) for p in range(nx)])


def relative_scatter(term):
    nz, nx = grid_of(lax.axis_size("gy"))
    order = z_order(nz)
    rows = term.shape[0] // (nz * nx)
    arrived, own = [], None
    for at in reversed(range(nz)):
        k = order[at]
        first = at * nx * rows
        total = term[first : first + rows].astype(F32)
        for p in range(1, nx):
            total = total + moved(term[first + p * rows : first + (p + 1) * rows], 0, p).astype(F32)
        if k:
            arrived.append(moved(total.astype(BF), k, 0))
        else:
            own = total
    for value in arrived:
        own = own + value.astype(F32)
    return own


def absolute_rows(value):
    nz, nx = grid_of(lax.axis_size("gy"))
    me = lax.axis_index("gy")
    z, x = me // nx, me % nx
    blocks = value.reshape(nz, nx, value.shape[0] // (nz * nx), value.shape[1])
    order = z_order(nz)
    turn = [order.index(k) for k in range(nz)]
    blocks = jnp.stack([blocks[at] for at in turn + turn])
    blocks = lax.dynamic_slice_in_dim(blocks, (nz - z) % nz, nz, 0)
    blocks = lax.dynamic_slice_in_dim(jnp.concatenate([blocks] * 2, 1), (nx - x) % nx, nx, 1)
    return blocks.reshape(value.shape)


def send_weight(weight):
    count = lax.axis_size("gx")
    found = [weight]
    for j in range(1, count // 2):
        found.append(lax.ppermute(weight, "gx", [(i, (i - 2 * j) % count) for i in range(count)]))
    return found


def pieces_of(found):
    count = lax.axis_size("gx")
    pieces = []
    for along in found:
        pieces += [along, lax.ppermute(along, "gx", [(i, i ^ 1) for i in range(count)])]
    return pieces


def piece_spots():
    count = lax.axis_size("gx")
    me = lax.axis_index("gx")
    spots = []
    for j in range(count // 2):
        along = (me + 2 * j) % count
        spots += [along, along ^ 1]
    return jnp.stack(spots).astype(jnp.int32)


def load_pieces(spots, pieces, whole, sems):
    copies = []
    for at, piece in enumerate(pieces):
        rows = piece.shape[0]
        first = pl.multiple_of(spots[at] * rows, 16) if len(pieces) > 1 else 0
        copy = pltpu.make_async_copy(piece, whole.at[pl.ds(first, rows)], sems.at[at])
        copy.start()
        copies.append(copy)
    return copies


def product_kernel(norm, counts, tile, spots, rows_ref, gain_ref, *refs):
    pieces, (out_ref, whole, sems) = refs[: counts[0]], refs[counts[0] :]
    for copy in load_pieces(spots, pieces, whole, sems):
        copy.wait()

    @pl.loop(0, rows_ref.shape[0] // tile)
    def _(step):
        span = pl.ds(pl.multiple_of(step * tile, 16), tile)
        normed = norm(rows_ref[span, :], gain_ref[...]).astype(BF)
        out_ref[span, :] = jnp.dot(normed, whole[...], preferred_element_type=F32).astype(BF)


def block_kernel(norm, counts, tile, spots, rows_ref, gain_ref, *refs):
    ups, downs = refs[: counts[0]], refs[counts[0] : sum(counts)]
    out_ref, up, down, up_sems, down_sems = refs[sum(counts) :]
    up_copies = load_pieces(spots, ups, up, up_sems)
    down_copies = load_pieces(spots, downs, down, down_sems)
    for copy in up_copies + down_copies:
        copy.wait()

    @pl.loop(0, rows_ref.shape[0] // tile)
    def _(step):
        span = pl.ds(pl.multiple_of(step * tile, 16), tile)
        normed = norm(rows_ref[span, :], gain_ref[...]).astype(BF)
        raised = jnp.dot(normed, up[...], preferred_element_type=F32)
        hidden = (0.5 * raised * (1.0 + lax.erf(raised * math.sqrt(0.5)))).astype(BF)
        out_ref[span, :] = lax.dot_general(
            hidden, down[...], (((1,), (1,)), ((), ())), preferred_element_type=F32
        ).astype(BF)


def tile_of(rows):
    return max(size for size in range(16, 321, 16) if rows % size == 0)


def pieces_call(kernel, norm, rows, gain, groups, columns, flops):
    counts = [len(group) for group in groups]
    wholes = [(group[0].shape[0] * len(group), group[0].shape[1]) for group in groups]
    spec = pl.BlockSpec(memory_space=pltpu.VMEM)
    return pl.pallas_call(
        functools.partial(kernel, norm, counts, tile_of(rows.shape[0])),
        out_shape=jax.ShapeDtypeStruct((rows.shape[0], columns), BF),
        grid_spec=pltpu.PrefetchScalarGridSpec(
            num_scalar_prefetch=1,
            grid=(),
            in_specs=[spec, spec] + [pl.BlockSpec(memory_space=pl.ANY)] * sum(counts),
            out_specs=spec,
            scratch_shapes=[pltpu.VMEM(shape, BF) for shape in wholes]
            + [pltpu.SemaphoreType.DMA((count,)) for count in counts],
        ),
        compiler_params=pltpu.CompilerParams(vmem_limit_bytes=40 * 1024 * 1024),
        cost_estimate=pl.CostEstimate(
            flops=flops,
            bytes_accessed=sum(2 * a * b for a, b in wholes) + 4 * rows.size,
            transcendentals=0,
        ),
    )(piece_spots(), rows, gain[None, :], *[piece for group in groups for piece in group])


def product_of(norm, rows, gain, pieces):
    columns = pieces[0].shape[1]
    return pieces_call(
        product_kernel, norm, rows, gain, [pieces], columns, 2 * rows.size * columns
    )


def block_of(norm, rows, gain, ups, downs):
    flops = 4 * rows.size * ups[0].shape[1]
    return pieces_call(block_kernel, norm, rows, gain, [ups, downs], rows.shape[1], flops)


def weight_block(weight):
    return lax.all_gather(weight, "gx", axis=0, tiled=True)


def tied(first, *later):
    return lax.optimization_barrier((first, *later))


def attend(joined, allowed):
    total = joined.shape[0]
    heads_here = joined.shape[1] // (3 * HEAD_DIM)
    grouped = joined.reshape(total, heads_here, 3, HEAD_DIM)
    query = grouped[:, :, 0]
    keys = grouped[:, :, 1]
    values = grouped[:, :, 2]
    scale = 1.0 / math.sqrt(HEAD_DIM)
    scores = jnp.einsum("qhe,khe->hqk", query, keys, preferred_element_type=F32) * scale
    scores = jnp.where(allowed[None], scores, -1e30)
    top = jnp.max(scores, axis=-1, keepdims=True)
    weights = jnp.exp(scores - top)
    probs = (weights / jnp.sum(weights, axis=-1, keepdims=True)).astype(BF)
    mixed = jnp.einsum("hqk,khe->qhe", probs, values, preferred_element_type=F32)
    return mixed.astype(BF).reshape(total, heads_here * HEAD_DIM)


def out_term(hidden, weight):
    return lax.dot_general(
        hidden, weight, (((1,), (1,)), ((), ())), preferred_element_type=F32
    ).astype(BF)


def shards(
    patches,
    prompt,
    image_ids,
    positions,
    norm_gains,
    vit_qkv,
    vit_out,
    vit_up,
    vit_down,
    merge_proj,
    dec_qkv,
    dec_out,
    dec_up,
    dec_down,
):
    local, width = patches.shape
    seq_local = prompt.shape[0]
    merged_rows = image_ids.shape[1]
    owner = relative_owner()
    window_of = (
        owner[:, None] * (local // 4) + jnp.arange(local // 4, dtype=jnp.int32)[None, :]
    ).reshape(-1)
    picks = window_of[:, None] == jnp.arange(merged_rows, dtype=jnp.int32)[None, :]
    labels = jnp.repeat(jnp.sum(jnp.where(picks, image_ids[0][None, :], 0), axis=1), 4)
    spots_of = (
        owner[:, None] * seq_local + jnp.arange(seq_local, dtype=jnp.int32)[None, :]
    ).reshape(-1)
    hits = positions[0][None, :] == spots_of[:, None]

    patch_found = start_gather(patches)
    sent_qkv = send_weight(vit_qkv)
    sent_down = send_weight(vit_down)
    outs_block = weight_block(jnp.concatenate([vit_out, dec_out], axis=1))
    qkvs = pieces_of(sent_qkv)
    patch_all = finish_gather(patch_found)
    enc_qkv = product_of(layer_norm, patch_all, norm_gains[0], qkvs)
    enc_qkv, outs_block, vit_up, prompt = tied(enc_qkv, outs_block, vit_up, prompt)
    up_block = weight_block(vit_up)
    columns = vit_out.shape[1]
    out_block, dout_block = outs_block[:, :columns], outs_block[:, columns:]
    prompt_found = start_z(prompt)
    enc_mix = attend(enc_qkv, labels[:, None] == labels[None, :])
    summed = relative_scatter(out_term(enc_mix, out_block))
    enc_mid = (patches.astype(F32) + summed).astype(BF)
    enc_mid, up_block, merge_proj, sent_down = tied(enc_mid, up_block, merge_proj, sent_down)
    merge_block = weight_block(merge_proj)
    downs = pieces_of(sent_down)

    mid_all = relative_gather(enc_mid)
    mid_all, prompt_found = tied(mid_all, prompt_found)
    prompt_found = swap_x(prompt_found, 0)
    term = block_of(layer_norm, mid_all, norm_gains[1], [up_block], downs)
    enc_out = (enc_mid.astype(F32) + relative_scatter(term)).astype(BF)
    enc_out, merge_block, dec_qkv, prompt_found, dec_down = tied(
        enc_out, merge_block, dec_qkv, prompt_found, dec_down
    )
    dqkv_block = weight_block(dec_qkv)
    windows = layer_norm(enc_out, norm_gains[2]).astype(BF).reshape(local // 4, 4 * width)
    prompt_found = swap_x(prompt_found, 1)
    windows = relative_gather(windows)
    prompt_all = joined_blocks(prompt_found)
    merged = jnp.dot(windows, merge_block, preferred_element_type=F32).astype(BF)
    merged, dqkv_block, dec_up = tied(merged, dqkv_block, dec_up)
    dup_block = weight_block(dec_up)
    sent_ddown = send_weight(dec_down)
    merged = lax.dot_general(
        merged, picks.astype(BF), (((0,), (0,)), ((), ())), preferred_element_type=F32
    ).astype(BF)
    merged_all = absolute_rows(relative_gather(merged))

    placed = lax.dot_general(
        hits.astype(BF), merged_all, (((1,), (1,)), ((), ())), preferred_element_type=F32
    ).astype(BF)
    dec_all = jnp.where(jnp.any(hits, axis=1)[:, None], placed, prompt_all)
    dec_in = dec_all[:seq_local]
    dec_rows = product_of(rms_norm, dec_all, norm_gains[3], [dqkv_block])
    dec_mix = attend(dec_rows, spots_of[:, None] >= spots_of[None, :])
    summed = relative_scatter(out_term(dec_mix, dout_block))
    dec_mid = (dec_in.astype(F32) + summed).astype(BF)
    dec_mid, dup_block, sent_ddown = tied(dec_mid, dup_block, sent_ddown)
    ddowns = pieces_of(sent_ddown)

    mid_all = relative_gather(dec_mid)
    term = block_of(rms_norm, mid_all, norm_gains[4], [dup_block], ddowns)
    return (dec_mid.astype(F32) + relative_scatter(term)).astype(BF)


def solution(mesh):
    weight = P("gx", "gy")
    rows = P(("gx", "gy"), None)
    in_specs = (rows, rows, P("gx", None), P("gx", None), P()) + (weight,) * 9
    return jax.shard_map(shards, mesh=mesh, in_specs=in_specs, out_specs=rows, check_vma=False)
```

```python
import functools
import math

import jax
import jax.numpy as jnp
from jax import lax
from jax.experimental import pallas as pl
from jax.experimental.pallas import tpu as pltpu
from jax.sharding import PartitionSpec as P

HEAD_DIM = 104
BF = jnp.bfloat16
F32 = jnp.float32


def layer_norm(rows, gain):
    values = rows.astype(F32)
    center = values - jnp.mean(values, axis=-1, keepdims=True)
    spread = jnp.mean(center * center, axis=-1, keepdims=True)
    return center * lax.rsqrt(spread + 1e-06) * gain


def rms_norm(rows, gain):
    values = rows.astype(F32)
    return values * lax.rsqrt(jnp.mean(values * values, axis=-1, keepdims=True) + 1e-06) * gain


def grid_of(count):
    fast = 2 ** ((count.bit_length() - 1) // 2)
    return count // fast, fast


def moved(value, dz, dx):
    nz, nx = grid_of(lax.axis_size("gy"))
    pairs = [
        (z * nx + x, ((z + dz) % nz) * nx + (x + dx) % nx) for z in range(nz) for x in range(nx)
    ]
    return lax.ppermute(value, "gy", pairs)


def z_order(nz):
    return sorted(range(nz), key=lambda k: (min(k, nz - k), k))


def start_z(value):
    nz, nx = grid_of(lax.axis_size("gy"))
    found = {(0, 0): value}
    for k in z_order(nz)[1:]:
        found[k, 0] = moved(value, -k, 0)
    return found


def swap_x(found, half):
    nz, nx = grid_of(lax.axis_size("gy"))
    found = dict(found)
    for k in z_order(nz)[half * nz // 2 : (half + 1) * nz // 2]:
        for p in range(1, nx):
            found[k, p] = moved(found[k, 0], 0, -p)
    return found


def joined_blocks(found):
    nz, nx = grid_of(lax.axis_size("gy"))
    return jnp.concatenate([found[k, p] for k in z_order(nz) for p in range(nx)], axis=0)


def start_gather(value):
    nz, nx = grid_of(lax.axis_size("gy"))
    found = start_z(value)
    for p in range(1, nx):
        found[0, p] = moved(value, 0, -p)
    return found


def finish_gather(found):
    nz, nx = grid_of(lax.axis_size("gy"))
    found = dict(found)
    for k in z_order(nz)[1:]:
        for p in range(1, nx):
            found[k, p] = moved(found[k, 0], 0, -p)
    return joined_blocks(found)


def relative_gather(value):
    return finish_gather(start_gather(value))


def relative_owner():
    nz, nx = grid_of(lax.axis_size("gy"))
    me = lax.axis_index("gy")
    z, x = me // nx, me % nx
    return jnp.stack([((z + k) % nz) * nx + (x + p) % nx for k in z_order(nz) for p in range(nx)])


def relative_scatter(terms, late=None):
    nz, nx = grid_of(lax.axis_size("gy"))
    order = z_order(nz)
    swapped = {}
    for at in reversed(range(nz)):
        swapped[at] = [moved(terms[at * nx + p], 0, p) for p in range(1, nx)]
    arrived = []
    for at in reversed(range(1, nz)):
        last = added(terms[at * nx], *swapped[at])
        arrived.append(moved(last, order[at], 0))
    total = terms[0].astype(F32)
    for value in swapped[0] + arrived:
        total = total + value.astype(F32)
    return total if late is None else (total, after(late, last))


def after(value, first):
    return lax.optimization_barrier((value, first))[0]


def far_z():
    return z_order(grid_of(lax.axis_size("gy"))[0])[-1]


def absolute_rows(value):
    nz, nx = grid_of(lax.axis_size("gy"))
    me = lax.axis_index("gy")
    z, x = me // nx, me % nx
    blocks = value.reshape(nz, nx, value.shape[0] // (nz * nx), value.shape[1])
    order = z_order(nz)
    turn = [order.index(k) for k in range(nz)]
    blocks = jnp.stack([blocks[at] for at in turn + turn])
    blocks = lax.dynamic_slice_in_dim(blocks, (nz - z) % nz, nz, 0)
    blocks = lax.dynamic_slice_in_dim(jnp.concatenate([blocks] * 2, 1), (nx - x) % nx, nx, 1)
    return blocks.reshape(value.shape)


def send_weight(weight):
    count = lax.axis_size("gx")
    found = [weight]
    for j in range(1, count // 2):
        found.append(lax.ppermute(weight, "gx", [(i, (i - 2 * j) % count) for i in range(count)]))
    return found


def pieces_of(found):
    count = lax.axis_size("gx")
    pieces = []
    for along in found:
        pieces += [along, lax.ppermute(along, "gx", [(i, i ^ 1) for i in range(count)])]
    return pieces


def piece_spots():
    count = lax.axis_size("gx")
    me = lax.axis_index("gx")
    spots = []
    for j in range(count // 2):
        along = (me + 2 * j) % count
        spots += [along, along ^ 1]
    return jnp.stack(spots).astype(jnp.int32)


def load_pieces(spots, pieces, whole, sems):
    copies = []
    for at, piece in enumerate(pieces):
        rows = piece.shape[0]
        first = pl.multiple_of(spots[at] * rows, 16) if len(pieces) > 1 else 0
        copy = pltpu.make_async_copy(piece, whole.at[pl.ds(first, rows)], sems.at[at])
        copy.start()
        copies.append(copy)
    return copies


def product_kernel(norm, counts, tile, spots, rows_ref, gain_ref, *refs):
    pieces, (out_ref, whole, sems) = refs[: counts[0]], refs[counts[0] :]
    for copy in load_pieces(spots, pieces, whole, sems):
        copy.wait()

    @pl.loop(0, rows_ref.shape[0] // tile)
    def _(step):
        span = pl.ds(pl.multiple_of(step * tile, 16), tile)
        normed = norm(rows_ref[span, :], gain_ref[...]).astype(BF)
        out_ref[span, :] = jnp.dot(normed, whole[...], preferred_element_type=F32).astype(BF)


def store_blocks(out_refs, step, value):
    rows = out_refs[0].shape[0]
    tile = value.shape[0] // rows
    for at in range(tile):
        out_refs[step * tile + at][...] = value[at * rows : (at + 1) * rows].astype(BF)


def block_kernel(norm, counts, tile, spots, rows_ref, gain_ref, *refs):
    ups, downs = refs[: counts[0]], refs[counts[0] : sum(counts)]
    out_refs, (up, down, up_sems, down_sems) = refs[sum(counts) : -4], refs[-4:]
    up_copies = load_pieces(spots, ups, up, up_sems)
    down_copies = load_pieces(spots, downs, down, down_sems)
    for copy in up_copies + down_copies:
        copy.wait()
    for step in range(rows_ref.shape[0] // tile):
        normed = norm(rows_ref[step * tile : (step + 1) * tile, :], gain_ref[...]).astype(BF)
        raised = jnp.dot(normed, up[...], preferred_element_type=F32)
        hidden = (0.5 * raised * (1.0 + lax.erf(raised * math.sqrt(0.5)))).astype(BF)
        value = lax.dot_general(
            hidden, down[...], (((1,), (1,)), ((), ())), preferred_element_type=F32
        )
        store_blocks(out_refs, step, value)


def out_kernel(tile, mix_ref, weight_ref, *out_refs):
    for step in range(mix_ref.shape[0] // tile):
        value = lax.dot_general(
            mix_ref[step * tile : (step + 1) * tile, :],
            weight_ref[...],
            (((1,), (1,)), ((), ())),
            preferred_element_type=F32,
        )
        store_blocks(out_refs, step, value)


def add_kernel(*refs):
    total = refs[0][...].astype(F32)
    for ref in refs[1:-1]:
        total = total + ref[...].astype(F32)
    refs[-1][...] = total.astype(BF)


def added(*values):
    return pl.pallas_call(
        add_kernel,
        out_shape=jax.ShapeDtypeStruct(values[0].shape, BF),
        cost_estimate=pl.CostEstimate(
            flops=values[0].size, bytes_accessed=6 * values[0].size, transcendentals=0
        ),
    )(*values)


def block_tile(total):
    count = lax.axis_size("gy")
    rows = total // count
    return rows * max(size for size in range(1, count + 1) if count % size == 0 and rows * size <= 320)


def out_term(mix, weight):
    count = lax.axis_size("gy")
    total, columns = mix.shape[0], weight.shape[0]
    return pl.pallas_call(
        functools.partial(out_kernel, block_tile(total)),
        out_shape=[jax.ShapeDtypeStruct((total // count, columns), BF)] * count,
        compiler_params=pltpu.CompilerParams(vmem_limit_bytes=40 * 1024 * 1024),
        cost_estimate=pl.CostEstimate(
            flops=2 * mix.size * columns,
            bytes_accessed=2 * (mix.size + weight.size + total * columns),
            transcendentals=0,
        ),
    )(mix, weight)


def tile_of(rows):
    return max(size for size in range(16, 321, 16) if rows % size == 0)


def pieces_call(kernel, norm, rows, gain, groups, tile, outs, flops):
    counts = [len(group) for group in groups]
    wholes = [(group[0].shape[0] * len(group), group[0].shape[1]) for group in groups]
    spec = pl.BlockSpec(memory_space=pltpu.VMEM)
    return pl.pallas_call(
        functools.partial(kernel, norm, counts, tile),
        out_shape=[jax.ShapeDtypeStruct(shape, BF) for shape in outs],
        grid_spec=pltpu.PrefetchScalarGridSpec(
            num_scalar_prefetch=1,
            grid=(),
            in_specs=[spec, spec] + [pl.BlockSpec(memory_space=pl.ANY)] * sum(counts),
            out_specs=[spec] * len(outs),
            scratch_shapes=[pltpu.VMEM(shape, BF) for shape in wholes]
            + [pltpu.SemaphoreType.DMA((count,)) for count in counts],
        ),
        compiler_params=pltpu.CompilerParams(vmem_limit_bytes=40 * 1024 * 1024),
        cost_estimate=pl.CostEstimate(
            flops=flops,
            bytes_accessed=sum(2 * a * b for a, b in wholes) + 4 * rows.size,
            transcendentals=0,
        ),
    )(piece_spots(), rows, gain[None, :], *[piece for group in groups for piece in group])


def product_of(norm, rows, gain, pieces):
    total, columns = rows.shape[0], pieces[0].shape[1]
    flops = 2 * rows.size * columns
    return pieces_call(
        product_kernel, norm, rows, gain, [pieces], tile_of(total), [(total, columns)], flops
    )[0]


def block_of(norm, rows, gain, ups, downs):
    count = lax.axis_size("gy")
    total, width = rows.shape
    flops = 4 * rows.size * ups[0].shape[1]
    outs = [(total // count, width)] * count
    return pieces_call(
        block_kernel, norm, rows, gain, [ups, downs], block_tile(total), outs, flops
    )


def weight_block(weight):
    return lax.all_gather(weight, "gx", axis=0, tiled=True)


def tied(first, *later):
    return lax.optimization_barrier((first, *later))


def attend(joined, allowed):
    total = joined.shape[0]
    heads_here = joined.shape[1] // (3 * HEAD_DIM)
    grouped = joined.reshape(total, heads_here, 3, HEAD_DIM)
    query = grouped[:, :, 0]
    keys = grouped[:, :, 1]
    values = grouped[:, :, 2]
    scale = 1.0 / math.sqrt(HEAD_DIM)
    scores = jnp.einsum("qhe,khe->hqk", query, keys, preferred_element_type=F32) * scale
    scores = jnp.where(allowed[None], scores, -1e30)
    top = jnp.max(scores, axis=-1, keepdims=True)
    weights = jnp.exp(scores - top)
    probs = (weights / jnp.sum(weights, axis=-1, keepdims=True)).astype(BF)
    mixed = jnp.einsum("hqk,khe->qhe", probs, values, preferred_element_type=F32)
    return mixed.astype(BF).reshape(total, heads_here * HEAD_DIM)


def shards(
    patches,
    prompt,
    image_ids,
    positions,
    norm_gains,
    vit_qkv,
    vit_out,
    vit_up,
    vit_down,
    merge_proj,
    dec_qkv,
    dec_out,
    dec_up,
    dec_down,
):
    local, width = patches.shape
    seq_local = prompt.shape[0]
    merged_rows = image_ids.shape[1]
    owner = relative_owner()
    window_of = (
        owner[:, None] * (local // 4) + jnp.arange(local // 4, dtype=jnp.int32)[None, :]
    ).reshape(-1)
    picks = window_of[:, None] == jnp.arange(merged_rows, dtype=jnp.int32)[None, :]
    labels = jnp.repeat(jnp.sum(jnp.where(picks, image_ids[0][None, :], 0), axis=1), 4)
    spots_of = (
        owner[:, None] * seq_local + jnp.arange(seq_local, dtype=jnp.int32)[None, :]
    ).reshape(-1)
    hits = positions[0][None, :] == spots_of[:, None]

    patch_found = start_gather(patches)
    sent_qkv = send_weight(vit_qkv)
    outs_block = weight_block(jnp.concatenate([vit_out, dec_out], axis=1))
    qkvs = pieces_of(sent_qkv)
    patch_all = finish_gather(patch_found)
    enc_qkv = product_of(layer_norm, patch_all, norm_gains[0], qkvs)
    enc_qkv, outs_block, vit_up = tied(enc_qkv, outs_block, vit_up)
    up_block = weight_block(vit_up)
    columns = vit_out.shape[1]
    out_block, dout_block = outs_block[:, :columns], outs_block[:, columns:]
    enc_mix = attend(enc_qkv, labels[:, None] == labels[None, :])
    summed = relative_scatter(out_term(enc_mix, out_block))
    enc_mid = (patches.astype(F32) + summed).astype(BF)
    enc_mid, up_block, vit_down = tied(enc_mid, up_block, vit_down)
    down_block = weight_block(vit_down)

    mid_all = relative_gather(enc_mid)
    mid_all, down_block, merge_proj = tied(mid_all, down_block, merge_proj)
    merge_block = weight_block(merge_proj)
    term = block_of(layer_norm, mid_all, norm_gains[1], [up_block], [down_block])
    enc_out = (enc_mid.astype(F32) + relative_scatter(term)).astype(BF)
    enc_out, merge_block, dec_qkv = tied(enc_out, merge_block, dec_qkv)
    dqkv_block = weight_block(dec_qkv)
    windows = layer_norm(enc_out, norm_gains[2]).astype(BF).reshape(local // 4, 4 * width)
    windows = relative_gather(windows)
    merged = jnp.dot(windows, merge_block, preferred_element_type=F32).astype(BF)
    merged, dqkv_block, dec_up = tied(merged, dqkv_block, dec_up)
    dup_block = weight_block(dec_up)
    merged = lax.dot_general(
        merged, picks.astype(BF), (((0,), (0,)), ((), ())), preferred_element_type=F32
    ).astype(BF)
    merged_all = absolute_rows(relative_gather(merged))

    mine = hits[:seq_local]
    placed = lax.dot_general(
        mine.astype(BF), merged_all, (((1,), (1,)), ((), ())), preferred_element_type=F32
    ).astype(BF)
    dec_in = jnp.where(jnp.any(mine, axis=1)[:, None], placed, prompt)
    dec_all = relative_gather(dec_in)
    dec_rows = product_of(rms_norm, dec_all, norm_gains[3], [dqkv_block])
    dec_mix = attend(dec_rows, spots_of[:, None] >= spots_of[None, :])
    dec_mix, dup_block, dec_down = tied(dec_mix, dup_block, dec_down)
    ddown_block = weight_block(dec_down)
    summed = relative_scatter(out_term(dec_mix, dout_block))
    dec_mid = (dec_in.astype(F32) + summed).astype(BF)

    mid_all = relative_gather(dec_mid)
    term = block_of(rms_norm, mid_all, norm_gains[4], [dup_block], [ddown_block])
    return (dec_mid.astype(F32) + relative_scatter(term)).astype(BF)


def solution(mesh):
    weight = P("gx", "gy")
    rows = P(("gx", "gy"), None)
    in_specs = (rows, rows, P("gx", None), P("gx", None), P()) + (weight,) * 9
    return jax.shard_map(shards, mesh=mesh, in_specs=in_specs, out_specs=rows, check_vma=False)
```

```python
import functools
import math

import jax
import jax.numpy as jnp
from jax import lax
from jax.experimental import pallas as pl
from jax.experimental.pallas import tpu as pltpu
from jax.sharding import PartitionSpec as P

HEAD_DIM = 104
BF = jnp.bfloat16
F32 = jnp.float32


def layer_norm(rows, gain):
    values = rows.astype(F32)
    center = values - jnp.mean(values, axis=-1, keepdims=True)
    spread = jnp.mean(center * center, axis=-1, keepdims=True)
    return center * lax.rsqrt(spread + 1e-06) * gain


def rms_norm(rows, gain):
    values = rows.astype(F32)
    return values * lax.rsqrt(jnp.mean(values * values, axis=-1, keepdims=True) + 1e-06) * gain


def grid_of(count):
    fast = 2 ** ((count.bit_length() - 1) // 2)
    return count // fast, fast


def moved(value, dz, dx):
    nz, nx = grid_of(lax.axis_size("gy"))
    pairs = [
        (z * nx + x, ((z + dz) % nz) * nx + (x + dx) % nx) for z in range(nz) for x in range(nx)
    ]
    return lax.ppermute(value, "gy", pairs)


def z_order(nz):
    return sorted(range(nz), key=lambda k: (min(k, nz - k), k))


def start_z(value):
    nz, nx = grid_of(lax.axis_size("gy"))
    found = {(0, 0): value}
    for k in z_order(nz)[1:]:
        found[k, 0] = moved(value, -k, 0)
    return found


def swap_x(found, half):
    nz, nx = grid_of(lax.axis_size("gy"))
    found = dict(found)
    for k in z_order(nz)[half * nz // 2 : (half + 1) * nz // 2]:
        for p in range(1, nx):
            found[k, p] = moved(found[k, 0], 0, -p)
    return found


def joined_blocks(found):
    nz, nx = grid_of(lax.axis_size("gy"))
    return jnp.concatenate([found[k, p] for k in z_order(nz) for p in range(nx)], axis=0)


def start_gather(value):
    nz, nx = grid_of(lax.axis_size("gy"))
    found = start_z(value)
    for p in range(1, nx):
        found[0, p] = moved(value, 0, -p)
    return found


def finish_gather(found):
    nz, nx = grid_of(lax.axis_size("gy"))
    found = dict(found)
    for k in z_order(nz)[1:]:
        for p in range(1, nx):
            found[k, p] = moved(found[k, 0], 0, -p)
    return joined_blocks(found)


def relative_gather(value):
    return finish_gather(start_gather(value))


def relative_owner():
    nz, nx = grid_of(lax.axis_size("gy"))
    me = lax.axis_index("gy")
    z, x = me // nx, me % nx
    return jnp.stack([((z + k) % nz) * nx + (x + p) % nx for k in z_order(nz) for p in range(nx)])


def relative_scatter(terms, late=None):
    nz, nx = grid_of(lax.axis_size("gy"))
    order = z_order(nz)
    swapped = {}
    for at in reversed(range(nz)):
        swapped[at] = [moved(terms[at * nx + p], 0, p) for p in range(1, nx)]
    arrived = []
    for at in reversed(range(1, nz)):
        last = added(terms[at * nx], *swapped[at])
        arrived.append(moved(last, order[at], 0))
    total = terms[0].astype(F32)
    for value in swapped[0] + arrived:
        total = total + value.astype(F32)
    return total if late is None else (total, after(late, last))


def after(value, first):
    return lax.optimization_barrier((value, first))[0]


def far_z():
    return z_order(grid_of(lax.axis_size("gy"))[0])[-1]


def absolute_rows(value):
    nz, nx = grid_of(lax.axis_size("gy"))
    me = lax.axis_index("gy")
    z, x = me // nx, me % nx
    blocks = value.reshape(nz, nx, value.shape[0] // (nz * nx), value.shape[1])
    order = z_order(nz)
    turn = [order.index(k) for k in range(nz)]
    blocks = jnp.stack([blocks[at] for at in turn + turn])
    blocks = lax.dynamic_slice_in_dim(blocks, (nz - z) % nz, nz, 0)
    blocks = lax.dynamic_slice_in_dim(jnp.concatenate([blocks] * 2, 1), (nx - x) % nx, nx, 1)
    return blocks.reshape(value.shape)


def send_weight(weight):
    count = lax.axis_size("gx")
    found = [weight]
    for j in range(1, count // 2):
        found.append(lax.ppermute(weight, "gx", [(i, (i - 2 * j) % count) for i in range(count)]))
    return found


def pieces_of(found):
    count = lax.axis_size("gx")
    pieces = []
    for along in found:
        pieces += [along, lax.ppermute(along, "gx", [(i, i ^ 1) for i in range(count)])]
    return pieces


def piece_spots():
    count = lax.axis_size("gx")
    me = lax.axis_index("gx")
    spots = []
    for j in range(count // 2):
        along = (me + 2 * j) % count
        spots += [along, along ^ 1]
    return jnp.stack(spots).astype(jnp.int32)


def load_pieces(spots, pieces, whole, sems):
    copies = []
    for at, piece in enumerate(pieces):
        rows = piece.shape[0]
        first = pl.multiple_of(spots[at] * rows, 16) if len(pieces) > 1 else 0
        copy = pltpu.make_async_copy(piece, whole.at[pl.ds(first, rows)], sems.at[at])
        copy.start()
        copies.append(copy)
    return copies


def product_kernel(norm, counts, tile, spots, rows_ref, gain_ref, *refs):
    pieces, (out_ref, whole, sems) = refs[: counts[0]], refs[counts[0] :]
    for copy in load_pieces(spots, pieces, whole, sems):
        copy.wait()

    @pl.loop(0, rows_ref.shape[0] // tile)
    def _(step):
        span = pl.ds(pl.multiple_of(step * tile, 16), tile)
        normed = norm(rows_ref[span, :], gain_ref[...]).astype(BF)
        out_ref[span, :] = jnp.dot(normed, whole[...], preferred_element_type=F32).astype(BF)


def store_blocks(out_refs, step, value):
    rows = out_refs[0].shape[0]
    tile = value.shape[0] // rows
    for at in range(tile):
        out_refs[step * tile + at][...] = value[at * rows : (at + 1) * rows].astype(BF)


def block_kernel(norm, tile, rows_ref, gain_ref, up, down, *out_refs):
    for step in range(rows_ref.shape[0] // tile):
        normed = norm(rows_ref[step * tile : (step + 1) * tile, :], gain_ref[...]).astype(BF)
        raised = jnp.dot(normed, up[...], preferred_element_type=F32)
        hidden = (0.5 * raised * (1.0 + lax.erf(raised * math.sqrt(0.5)))).astype(BF)
        value = lax.dot_general(
            hidden, down[...], (((1,), (1,)), ((), ())), preferred_element_type=F32
        )
        store_blocks(out_refs, step, value)


def out_kernel(tile, mix_ref, weight_ref, *out_refs):
    for step in range(mix_ref.shape[0] // tile):
        value = lax.dot_general(
            mix_ref[step * tile : (step + 1) * tile, :],
            weight_ref[...],
            (((1,), (1,)), ((), ())),
            preferred_element_type=F32,
        )
        store_blocks(out_refs, step, value)


def add_kernel(*refs):
    total = refs[0][...].astype(F32)
    for ref in refs[1:-1]:
        total = total + ref[...].astype(F32)
    refs[-1][...] = total.astype(BF)


def added(*values):
    return pl.pallas_call(
        add_kernel,
        out_shape=jax.ShapeDtypeStruct(values[0].shape, BF),
        cost_estimate=pl.CostEstimate(
            flops=values[0].size, bytes_accessed=6 * values[0].size, transcendentals=0
        ),
    )(*values)


def block_tile(total):
    count = lax.axis_size("gy")
    rows = total // count
    return rows * max(size for size in range(1, count + 1) if count % size == 0 and rows * size <= 320)


def out_term(mix, weight):
    count = lax.axis_size("gy")
    total, columns = mix.shape[0], weight.shape[0]
    return pl.pallas_call(
        functools.partial(out_kernel, block_tile(total)),
        out_shape=[jax.ShapeDtypeStruct((total // count, columns), BF)] * count,
        compiler_params=pltpu.CompilerParams(vmem_limit_bytes=40 * 1024 * 1024),
        cost_estimate=pl.CostEstimate(
            flops=2 * mix.size * columns,
            bytes_accessed=2 * (mix.size + weight.size + total * columns),
            transcendentals=0,
        ),
    )(mix, weight)


def tile_of(rows):
    return max(size for size in range(16, 321, 16) if rows % size == 0)


def pieces_call(kernel, norm, rows, gain, groups, tile, outs, flops):
    counts = [len(group) for group in groups]
    wholes = [(group[0].shape[0] * len(group), group[0].shape[1]) for group in groups]
    spec = pl.BlockSpec(memory_space=pltpu.VMEM)
    return pl.pallas_call(
        functools.partial(kernel, norm, counts, tile),
        out_shape=[jax.ShapeDtypeStruct(shape, BF) for shape in outs],
        grid_spec=pltpu.PrefetchScalarGridSpec(
            num_scalar_prefetch=1,
            grid=(),
            in_specs=[spec, spec] + [pl.BlockSpec(memory_space=pl.ANY)] * sum(counts),
            out_specs=[spec] * len(outs),
            scratch_shapes=[pltpu.VMEM(shape, BF) for shape in wholes]
            + [pltpu.SemaphoreType.DMA((count,)) for count in counts],
        ),
        compiler_params=pltpu.CompilerParams(vmem_limit_bytes=40 * 1024 * 1024),
        cost_estimate=pl.CostEstimate(
            flops=flops,
            bytes_accessed=sum(2 * a * b for a, b in wholes) + 4 * rows.size,
            transcendentals=0,
        ),
    )(piece_spots(), rows, gain[None, :], *[piece for group in groups for piece in group])


def product_of(norm, rows, gain, pieces):
    total, columns = rows.shape[0], pieces[0].shape[1]
    flops = 2 * rows.size * columns
    return pieces_call(
        product_kernel, norm, rows, gain, [pieces], tile_of(total), [(total, columns)], flops
    )[0]


def block_of(norm, rows, gain, up, down):
    count = lax.axis_size("gy")
    total, width = rows.shape
    return pl.pallas_call(
        functools.partial(block_kernel, norm, block_tile(total)),
        out_shape=[jax.ShapeDtypeStruct((total // count, width), BF)] * count,
        compiler_params=pltpu.CompilerParams(vmem_limit_bytes=40 * 1024 * 1024),
        cost_estimate=pl.CostEstimate(
            flops=4 * rows.size * up.shape[1],
            bytes_accessed=2 * (up.size + down.size + 2 * rows.size),
            transcendentals=0,
        ),
    )(rows, gain[None, :], up, down)


def weight_block(weight):
    return lax.all_gather(weight, "gx", axis=0, tiled=True)


def tied(first, *later):
    return lax.optimization_barrier((first, *later))


def attend(joined, allowed):
    total = joined.shape[0]
    heads_here = joined.shape[1] // (3 * HEAD_DIM)
    grouped = joined.reshape(total, heads_here, 3, HEAD_DIM)
    query = grouped[:, :, 0]
    keys = grouped[:, :, 1]
    values = grouped[:, :, 2]
    scale = 1.0 / math.sqrt(HEAD_DIM)
    scores = jnp.einsum("qhe,khe->hqk", query, keys, preferred_element_type=F32) * scale
    scores = jnp.where(allowed[None], scores, -1e30)
    top = jnp.max(scores, axis=-1, keepdims=True)
    weights = jnp.exp(scores - top)
    probs = (weights / jnp.sum(weights, axis=-1, keepdims=True)).astype(BF)
    mixed = jnp.einsum("hqk,khe->qhe", probs, values, preferred_element_type=F32)
    return mixed.astype(BF).reshape(total, heads_here * HEAD_DIM)


def shards(
    patches,
    prompt,
    image_ids,
    positions,
    norm_gains,
    vit_qkv,
    vit_out,
    vit_up,
    vit_down,
    merge_proj,
    dec_qkv,
    dec_out,
    dec_up,
    dec_down,
):
    local, width = patches.shape
    seq_local = prompt.shape[0]
    merged_rows = image_ids.shape[1]
    owner = relative_owner()
    window_of = (
        owner[:, None] * (local // 4) + jnp.arange(local // 4, dtype=jnp.int32)[None, :]
    ).reshape(-1)
    picks = window_of[:, None] == jnp.arange(merged_rows, dtype=jnp.int32)[None, :]
    labels = jnp.repeat(jnp.sum(jnp.where(picks, image_ids[0][None, :], 0), axis=1), 4)
    spots_of = (
        owner[:, None] * seq_local + jnp.arange(seq_local, dtype=jnp.int32)[None, :]
    ).reshape(-1)
    hits = positions[0][None, :] == spots_of[:, None]

    patch_found = start_gather(patches)
    sent_qkv = send_weight(vit_qkv)
    outs_block = weight_block(jnp.concatenate([vit_out, dec_out], axis=1))
    qkvs = pieces_of(sent_qkv)
    patch_all = finish_gather(patch_found)
    enc_qkv = product_of(layer_norm, patch_all, norm_gains[0], qkvs)
    enc_qkv, outs_block, vit_up = tied(enc_qkv, outs_block, vit_up)
    up_block = weight_block(vit_up)
    columns = vit_out.shape[1]
    out_block, dout_block = outs_block[:, :columns], outs_block[:, columns:]
    enc_mix = attend(enc_qkv, labels[:, None] == labels[None, :])
    summed = relative_scatter(out_term(enc_mix, out_block))
    enc_mid = (patches.astype(F32) + summed).astype(BF)
    enc_mid, up_block, vit_down = tied(enc_mid, up_block, vit_down)
    down_block = weight_block(vit_down)

    mid_all = relative_gather(enc_mid)
    mid_all, down_block, merge_proj = tied(mid_all, down_block, merge_proj)
    merge_block = weight_block(merge_proj)
    term = block_of(layer_norm, mid_all, norm_gains[1], up_block, down_block)
    enc_out = (enc_mid.astype(F32) + relative_scatter(term)).astype(BF)
    enc_out, merge_block, dec_qkv = tied(enc_out, merge_block, dec_qkv)
    dqkv_block = weight_block(dec_qkv)
    windows = layer_norm(enc_out, norm_gains[2]).astype(BF).reshape(local // 4, 4 * width)
    windows = relative_gather(windows)
    merged = jnp.dot(windows, merge_block, preferred_element_type=F32).astype(BF)
    merged, dqkv_block, dec_up = tied(merged, dqkv_block, dec_up)
    dup_block = weight_block(dec_up)
    merged = lax.dot_general(
        merged, picks.astype(BF), (((0,), (0,)), ((), ())), preferred_element_type=F32
    ).astype(BF)
    merged_all = absolute_rows(relative_gather(merged))

    mine = hits[:seq_local]
    placed = lax.dot_general(
        mine.astype(BF), merged_all, (((1,), (1,)), ((), ())), preferred_element_type=F32
    ).astype(BF)
    dec_in = jnp.where(jnp.any(mine, axis=1)[:, None], placed, prompt)
    dec_all = relative_gather(dec_in)
    dec_rows = product_of(rms_norm, dec_all, norm_gains[3], [dqkv_block])
    dec_mix = attend(dec_rows, spots_of[:, None] >= spots_of[None, :])
    dec_mix, dup_block, dec_down = tied(dec_mix, dup_block, dec_down)
    ddown_block = weight_block(dec_down)
    summed = relative_scatter(out_term(dec_mix, dout_block))
    dec_mid = (dec_in.astype(F32) + summed).astype(BF)

    mid_all = relative_gather(dec_mid)
    term = block_of(rms_norm, mid_all, norm_gains[4], dup_block, ddown_block)
    return (dec_mid.astype(F32) + relative_scatter(term)).astype(BF)


def solution(mesh):
    weight = P("gx", "gy")
    rows = P(("gx", "gy"), None)
    in_specs = (rows, rows, P("gx", None), P("gx", None), P()) + (weight,) * 9
    return jax.shard_map(shards, mesh=mesh, in_specs=in_specs, out_specs=rows, check_vma=False)
```
